32 devices in a mesh: segment: 2 (over y), expert: 4 (over x, core), dp: 4 (over z).
Axes of the slice: x: 2, y: 2, z: 4, core: 2. Of those that a mesh axis runs over, the one named last changes fastest.
Arguments:
- tokens: bfloat16 [2, 2048, 3072], P(None, ('segment', 'expert', 'dp')), may hold values from -6 to 6
- routes: int32 [2, 2048, 2], P(None, ('segment', 'expert', 'dp')), may hold values from 0 to 3, all different within a row; in each aligned block of 64 rows (0 to 63, 64 to 127, ..., all dimensions but the last counted through in order) at most 34 rows name the same one
- combine: float32 [2, 2048, 2], P(None, ('segment', 'expert', 'dp')), may hold values from 0.2 to 1
- expert_home: int32 [4], replicated, may hold values from 0 to 3, each once
- up_weight: bfloat16 [2, 4, 8192, 3072], P('segment', 'expert', 'dp'), may hold values from -0.109375 to 0.109375
- down_weight: bfloat16 [2, 4, 8192, 3072], P('segment', 'expert', 'dp'), may hold values from -0.0625 to 0.0625
Outputs:
- received: bfloat16 [2, 2048, 3072], P(None, ('segment', 'expert', 'dp'))
The draws below stay inside these ranges and needn't reach their ends.
Inputs may be any that keep to these rules, and one draw needn't show every extreme that they name: `routes`: each token names 2 different experts. In each micro-batch the 64 tokens of one device name one expert at most 34 times. `expert_home`: every home holds exactly one expert.
All inputs are finite; a program needn't handle non-finite values.
Results may differ from the reference program's by a relative error of at most 0.0065.
Values may be sent and summed in bfloat16 or wider, within the bound.
No kernel may reach another device: no remote copies, remote signals or barrier semaphores. Data moves between devices by JAX's collectives and lax.ppermute only.
A program may use at most 128 MiB of HBM per device.

```python
import math
import jax
import jax.numpy as jnp
import numpy as np
from jax import lax

D = 3072
FF = 8192
TOP = 2
MB = 2
TOK_DEV = 64
EXPERTS = 4
TOKENS = 2048
MOST = 34
N_SEGMENT = 2
N_EXPERT = 4
N_DP = 4


def block_scale(key, dims, cuts, smallest, high):
    def one(axis_at, blocks):
        draws = jax.random.uniform(jax.random.fold_in(jax.random.fold_in(key, 6), axis_at), (blocks,), jnp.float32, smallest / len(cuts), high / len(cuts))
        return jnp.repeat(jnp.exp(draws), dims[axis_at] // blocks).reshape((-1,) + (1,) * (len(dims) - axis_at - 1))

    factor_of = one(*cuts[0])
    for cut in cuts[1:]:
        factor_of = factor_of * one(*cut)
    return factor_of


def shared_out(own_key, own, number, rows, count, top, bound, slope):
    ranking = jax.random.permutation(own_key, count)
    heavy_load, usual = load_shares(count, rows * top, bound, slope, True), load_shares(count, rows * top, bound, slope, False)
    places = jnp.arange(count)

    def named(sizes, rotation):
        used = int((sizes > 0).sum())
        fixed = max(1, used // 4)
        passed = fixed + (places - fixed + rotation * (used - fixed)) % max(1, count - fixed)
        return jnp.zeros((count,), jnp.int32).at[ranking[jnp.where(places < fixed, places, passed)]].set(jnp.asarray(sizes, jnp.int32))

    sizes = jnp.where(number % 4 == 0, named(heavy_load, number // 4), named(usual, number - number // 4 - 1))
    mixed = jax.random.permutation(jax.random.fold_in(own, 3), count)
    giver, taker = mixed[0:count // 2 * 2:2], mixed[1:count // 2 * 2:2]
    margin = jnp.minimum(sizes[giver] - 1, bound - sizes[taker]) // 2
    margin = jnp.where((giver == ranking[0]) | (taker == ranking[0]) | (sizes[taker] == 0), 0, jnp.maximum(margin, 0))
    passed = jax.random.randint(jax.random.fold_in(own, 4), (count // 2,), 0, 1 << 20) % (margin + 1)
    sizes = sizes.at[giver].add(-passed).at[taker].add(passed)
    labels = jnp.searchsorted(jnp.cumsum(sizes), jnp.arange(rows * top), side="right").astype(jnp.int32)
    listing = labels.reshape(top, rows).T
    listing = listing[jax.random.permutation(jax.random.fold_in(own, 1), rows)]
    rotation = jax.random.randint(jax.random.fold_in(own, 2), (rows, 1), 0, top)
    return jnp.take_along_axis(listing, (jnp.arange(top)[None, :] + rotation) % top, axis=1)


def load_shares(count, total, most, slope, full):
    weights = [(1 << 20) // math.isqrt(rank ** slope) + 1 for rank in range(1, count + 1)]
    largest = most if full else min(most, max(-(-total // count), total * weights[0] // sum(weights)))
    least = 1 if total - largest >= count - 1 else 0
    holding, rest = [largest] + [least] * (count - 1), total - largest - least * (count - 1)
    while rest > 0:
        movable = [i for i in range(1, count) if holding[i] < largest] or [i for i in range(1, count) if holding[i] < most]
        pool, left = sum([weights[i] for i in movable]), rest
        for i in movable:
            more = min(most - holding[i], max(1, left * weights[i] // pool), rest)
            holding[i] = holding[i] + more
            rest = rest - more
    return np.array(holding)


def centred(rng, dims, spread, reach, pieces=(), kind=jnp.bfloat16):
    values = jax.random.normal(rng, dims, jnp.float32) * spread
    if len(pieces) > 0:
        values = block_scale(rng, dims, pieces, -0.22, 0.18) * values
    return jnp.clip(values, min=-reach, max=reach).astype(kind)


def setup_inputs(seed: int = 0) -> dict:
    streams_of = jax.random.split(jax.random.key(seed), 7)
    tokens = centred(streams_of[0], (MB, TOKENS, D), 1.0, 6.0, ((1, 32),))
    routes_keys = jax.random.split(jax.random.fold_in(streams_of[1], 1), MB * TOKENS // TOK_DEV)
    routes_turns = jax.random.permutation(jax.random.fold_in(streams_of[1], 3), MB * TOKENS // TOK_DEV)
    routes = jax.vmap(lambda own, number: shared_out(jax.random.fold_in(streams_of[1], 2), own, number, TOK_DEV, EXPERTS, TOP, MOST, 1))(routes_keys, routes_turns).reshape((MB, TOKENS, TOP))
    combine = jnp.clip(0.2 + 0.8 * jax.random.uniform(streams_of[2], (MB, TOKENS, TOP), jnp.float32) ** block_scale(streams_of[2], (MB, TOKENS, TOP), ((1, 32),), -0.2, 0.2), 0.2, 1.0)
    expert_home = jax.random.permutation(streams_of[3], EXPERTS).astype(jnp.int32)
    up_weight = centred(streams_of[4], (N_SEGMENT, EXPERTS, FF, D), D ** -0.5, 0.109375, ((0, 2), (1, 4), (2, 4)))
    down_weight = centred(streams_of[5], (N_SEGMENT, EXPERTS, FF, D), FF ** -0.5, 0.0625, ((0, 2), (1, 4), (2, 4)))
    return {"tokens": tokens, "routes": routes, "combine": combine, "expert_home": expert_home, "up_weight": up_weight, "down_weight": down_weight}


def expert_rows(row_block, up_rows, down_rows):
    pre_act = lax.dot_general(row_block, up_rows, (((1,), (1,)), ((), ())), preferred_element_type=jnp.float32)
    hidden = jax.nn.silu(pre_act).astype(jnp.bfloat16)
    share = FF // N_DP
    total = jnp.zeros((row_block.shape[0], down_rows.shape[1]), jnp.float32)
    for share_index in range(N_DP):
        first = share_index * share
        piece = jnp.dot(hidden[:, first:first + share], down_rows[first:first + share], preferred_element_type=jnp.float32)
        rounded = lax.optimization_barrier(piece.astype(jnp.bfloat16))
        total = total + rounded.astype(jnp.float32)
    return total.astype(jnp.bfloat16)


def segment_layer(block_tokens, block_routes, block_combine, expert_home, up_segment, down_segment):
    pair_total = block_routes.shape[0] * TOP
    chosen = block_routes.reshape(-1).astype(jnp.int32)
    expert_ids = jnp.arange(EXPERTS, dtype=jnp.int32)
    onehot = (chosen[:, None] == expert_ids[None, :]).astype(jnp.int32)
    before = jnp.cumsum(onehot, axis=0) - onehot
    position = jnp.sum(before * onehot, axis=1).astype(jnp.int32)
    limit = MOST * N_EXPERT * N_DP
    slot_index = (chosen * limit + position).astype(jnp.int32)
    owner_of = (jnp.arange(pair_total, dtype=jnp.int32) // TOP).astype(jnp.int32)
    packed = jnp.zeros((EXPERTS * limit, D), jnp.bfloat16).at[slot_index].set(block_tokens[owner_of])
    packed = packed.reshape(EXPERTS, limit, D)

    def one_expert(expert_index):
        home_index = expert_home[expert_index].astype(jnp.int32)
        rows_in = lax.dynamic_index_in_dim(packed, expert_index, 0, keepdims=False)
        up_rows = lax.dynamic_index_in_dim(up_segment, home_index, 0, keepdims=False)
        down_rows = lax.dynamic_index_in_dim(down_segment, home_index, 0, keepdims=False)
        return expert_rows(rows_in, up_rows, down_rows)

    served = lax.map(one_expert, expert_ids)
    answers = served.reshape(EXPERTS * limit, D)[slot_index].astype(jnp.float32).reshape(-1, TOP, D)
    return jnp.sum(answers * block_combine[:, :, None], axis=1).astype(jnp.bfloat16)


def reference(tokens, routes, combine, expert_home, up_weight, down_weight):
    per_segment = TOKENS // N_SEGMENT
    batch_outs = []
    for batch_index in range(MB):
        segment_outs = []
        for segment_index in range(N_SEGMENT):
            first_row = segment_index * per_segment
            last_row = first_row + per_segment
            segment_outs.append(segment_layer(tokens[batch_index, first_row:last_row], routes[batch_index, first_row:last_row], combine[batch_index, first_row:last_row], expert_home, up_weight[segment_index], down_weight[segment_index]))
        blended = jnp.concatenate([segment_outs[-1]] + segment_outs[:-1], axis=0)
        batch_outs.append(blended)
    return jnp.stack(batch_outs, axis=0)
```

```python
import jax
import jax.numpy as jnp
from jax import lax
from jax.sharding import PartitionSpec as P


def passed_along(block, axis, distance):
    devices = range(lax.axis_size(axis))
    route = [((i - distance) % len(devices), i) for i in devices]
    return lax.ppermute(block, axis, route)


def swapped(block, axis, bits):
    return lax.ppermute(block, axis, [(i, i ^ bits) for i in range(lax.axis_size(axis))])


def placed_pairs(routes, expert_home):
    first, second = routes[:, 0], routes[:, 1]
    count = routes.shape[0]
    earlier = jnp.arange(count)[:, None] < jnp.arange(count)[None, :]
    rank_first = jnp.sum(jnp.where(earlier & (first[:, None] == first[None, :]), 1, 0), axis=0)
    rank_second = jnp.sum(
        jnp.where(first[:, None] == second[None, :], 1, 0)
        + jnp.where(earlier & (second[:, None] == second[None, :]), 1, 0),
        axis=0,
    )
    chosen = routes.T
    ids = jnp.arange(expert_home.shape[0], dtype=jnp.int32)
    home = jnp.sum(jnp.where(chosen[:, :, None] == ids, expert_home, 0), axis=-1)
    return home, jnp.stack([rank_first, rank_second])


def expert_share(rows, up_rows, down_rows):
    pre_act = lax.dot_general(
        rows, up_rows, (((1,), (1,)), ((), ())), preferred_element_type=jnp.float32
    )
    hidden = jax.nn.silu(pre_act).astype(jnp.bfloat16)
    return jnp.dot(hidden, down_rows, preferred_element_type=jnp.float32).astype(jnp.bfloat16)


def on_device(tokens, routes, combine, expert_home, up_weight, down_weight):
    up_rows = up_weight[0, 0]
    down_rows = down_weight[0, 0]
    batches, tok_rows, features = tokens.shape
    top_count = routes.shape[2]
    experts = expert_home.shape[0]
    sides = lax.axis_size("expert") // 2
    capacity = min(tok_rows, tok_rows * top_count // experts + tok_rows // 32)
    here = lax.axis_index("expert")
    side, core = here // 2, here % 2
    bf16, f32 = jnp.bfloat16, jnp.float32

    facts = []
    for m in range(batches):
        home, rank = placed_pairs(routes[m], expert_home)
        facts += [(home * tok_rows + rank).astype(f32), combine[m].T]
    facts = jnp.concatenate(facts)
    facts_far = jnp.stack([facts, swapped(facts, "dp", 2)])
    facts_own = jnp.stack([facts_far, swapped(facts_far, "dp", 1)])
    facts_all = jnp.stack([facts_own] + [swapped(facts_own, "expert", 2 * j) for j in range(1, sides)])
    facts_all = facts_all.reshape(sides, 2, 2, batches, 2, top_count, tok_rows)

    group_rows = sides * 2 * capacity
    group_tokens = sides * 2 * tok_rows

    def slots_of(m, near):
        code = facts_all[:, near, :, m, 0].astype(jnp.int32)
        weight = facts_all[:, near, :, m, 1]
        home, rank = code // tok_rows, code % tok_rows
        block = (jnp.arange(sides)[:, None] * 2 + jnp.arange(2)[None, :])[:, :, None, None]
        slot = jnp.where(home % 2 == core, 0, group_rows) + block * capacity + rank
        slot = jnp.where(home // 2 == side, slot, -1)
        slot = slot.transpose(2, 0, 1, 3).reshape(top_count, group_tokens)
        return slot, weight.transpose(2, 0, 1, 3).reshape(top_count, group_tokens)

    def spread(m):
        own = tokens[m]
        column = jnp.stack([own, swapped(own, "dp", 2)])
        columns = [column, swapped(column, "dp", 1)]
        groups = []
        for column in columns:
            groups.append(
                jnp.concatenate([column] + [swapped(column, "expert", 2 * j) for j in range(1, sides)])
                .reshape(group_tokens, features)
            )
        return groups

    def served(m, near, group):
        slot, weight = slots_of(m, near)
        ids = jnp.arange(2 * group_rows)
        pick = sum((ids[:, None] == slot[k][None, :]).astype(bf16) for k in range(top_count))
        packed = jnp.dot(pick, group, preferred_element_type=f32).astype(bf16)
        mine, other = packed[:group_rows], packed[group_rows:]
        rows = jnp.concatenate([mine, swapped(other, "expert", 1)])
        answers = expert_share(rows, up_rows, down_rows)
        answers = jnp.concatenate(
            [answers[:group_rows], swapped(answers[group_rows:], "expert", 1)]
        )
        mix = sum(
            jnp.where(slot[k][:, None] == ids[None, :], weight[k][:, None], 0.0)
            for k in range(top_count)
        )
        high = mix.astype(bf16)
        low = (mix - high.astype(f32)).astype(bf16)
        out = jnp.dot(high, answers, preferred_element_type=f32)
        out = out + jnp.dot(low, answers, preferred_element_type=f32)
        out = out.reshape(sides, 2 * tok_rows, features)
        total = out[0]
        for j in range(1, sides):
            total = total + swapped(out[j].astype(bf16), "expert", 2 * j).astype(f32)
        return total

    groups = [spread(m) for m in range(batches)]
    results = []
    for m in range(batches):
        far = served(m, 1, groups[m][1])
        total = served(m, 0, groups[m][0]) + swapped(far.astype(bf16), "dp", 1).astype(f32)
        back = swapped(total[tok_rows:].astype(bf16), "dp", 2)
        blended = (total[:tok_rows] + back.astype(f32)).astype(bf16)
        results.append(passed_along(blended, "segment", 1))
    return jnp.stack(results, axis=0)


def solution(mesh):
    return jax.shard_map(
        on_device,
        mesh=mesh,
        in_specs=(
            P(None, ("segment", "expert", "dp"), None),
            P(None, ("segment", "expert", "dp"), None),
            P(None, ("segment", "expert", "dp"), None),
            P(),
            P("segment", "expert", "dp", None),
            P("segment", "expert", "dp", None),
        ),
        out_specs=P(None, ("segment", "expert", "dp"), None),
        check_vma=False,
    )
```

```python
import functools

import jax
import jax.numpy as jnp
from jax import lax
from jax.experimental import pallas as pl
from jax.experimental.pallas import tpu as pltpu
from jax.sharding import PartitionSpec as P

BF16, F32 = jnp.bfloat16, jnp.float32


def passed_along(block, axis, distance):
    devices = range(lax.axis_size(axis))
    route = [((i - distance) % len(devices), i) for i in devices]
    return lax.ppermute(block, axis, route)


def swapped(block, axis, bits):
    return lax.ppermute(block, axis, [(i, i ^ bits) for i in range(lax.axis_size(axis))])


def placed_pairs(routes, expert_home):
    first, second = routes[:, 0], routes[:, 1]
    count = routes.shape[0]
    earlier = jnp.arange(count)[:, None] < jnp.arange(count)[None, :]
    rank_first = jnp.sum(jnp.where(earlier & (first[:, None] == first[None, :]), 1, 0), axis=0)
    rank_second = jnp.sum(
        jnp.where(first[:, None] == second[None, :], 1, 0)
        + jnp.where(earlier & (second[:, None] == second[None, :]), 1, 0),
        axis=0,
    )
    chosen = routes.T
    ids = jnp.arange(expert_home.shape[0], dtype=jnp.int32)
    home = jnp.sum(jnp.where(chosen[:, :, None] == ids, expert_home, 0), axis=-1)
    return home, jnp.stack([rank_first, rank_second])


def arrivals(sides, batch):
    steps = ((0,), (1, 2), (3,)) if batch == 0 else ((0,), (1, 2, 3))
    return [(j, bits) for step in steps for j in range(sides) for bits in step]


def departures(sides):
    return [(j, bits) for j in range(sides) for bits in (3, 1, 2, 0)]


def plan_kernel(sides, batches, top_count, capacity, half, place_ref, facts_ref, pick_ref, high_ref, low_ref):
    side, core = place_ref[0], place_ref[1]
    tok_rows = facts_ref.shape[-1]
    rows = 2 * half
    tokens = sides * 4 * tok_rows
    padded = -(-rows // 128) * 128
    ids = lax.broadcasted_iota(jnp.int32, (padded, tokens), 0)
    for m in range(batches):
        pick = jnp.zeros((rows, tokens), F32)
        mix = jnp.zeros((padded, tokens), F32)
        for k in range(top_count):
            slots, weights = {}, {}
            for j, bits in departures(sides):
                at = m * 2 * top_count + k
                code = facts_ref[j, bits, at : at + 1, :].astype(jnp.int32)
                at = at + top_count
                weights[j, bits] = facts_ref[j, bits, at : at + 1, :]
                home, rank = code // tok_rows, code % tok_rows
                slot = (j * 4 + bits) * capacity + rank + jnp.where(home % 2 == core, 0, half)
                slots[j, bits] = jnp.where(home // 2 == side, slot, -1)
            hit = ids[:rows] == jnp.concatenate([slots[at] for at in arrivals(sides, m)], axis=1)
            pick = jnp.where(hit, 1.0, pick)
            hit = ids == jnp.concatenate([slots[at] for at in departures(sides)], axis=1)
            mix = jnp.where(hit, jnp.concatenate([weights[at] for at in departures(sides)], axis=1), mix)
        mix = mix.T[:, :rows]
        high = mix.astype(BF16)
        pick_ref[m] = pick.astype(BF16)
        high_ref[m] = high
        low_ref[m] = (mix - high.astype(F32)).astype(BF16)


def plan(place, facts, batches, top_count, capacity, half):
    sides, tok_rows = facts.shape[0], facts.shape[-1]
    shape = jax.ShapeDtypeStruct((batches, 2 * half, sides * 4 * tok_rows), BF16)
    mixed = jax.ShapeDtypeStruct((batches, sides * 4 * tok_rows, 2 * half), BF16)
    vmem = pl.BlockSpec(memory_space=pltpu.VMEM)
    return pl.pallas_call(
        functools.partial(plan_kernel, sides, batches, top_count, capacity, half),
        out_shape=[shape, mixed, mixed],
        in_specs=[pl.BlockSpec(memory_space=pltpu.SMEM), vmem],
        out_specs=[vmem] * 3,
        cost_estimate=pl.CostEstimate(
            flops=10 * shape.size, bytes_accessed=6 * shape.size, transcendentals=0
        ),
        compiler_params=pltpu.CompilerParams(vmem_limit_bytes=32 * 2**20),
    )(place, facts)


def expert_kernel(steps, half, mine_ref, other_ref, up_ref, down_ref, *refs):
    mine_out, other_out, rows, hidden = refs[-4:]
    step = pl.program_id(0)
    chunk = up_ref.shape[0]

    @pl.when(step == 0)
    def _():
        rows[:half] = mine_ref[...]
        rows[half:] = other_ref[...]

    for s in range(steps):

        @pl.when(step == s)
        def _():
            pre_act = lax.dot_general(
                rows[...], up_ref[...], (((1,), (1,)), ((), ())), preferred_element_type=F32
            )
            hidden[:, s * chunk : (s + 1) * chunk] = jax.nn.silu(pre_act).astype(BF16)

    @pl.when(step >= steps)
    def _():
        answer = jnp.dot(hidden[...], down_ref[...], preferred_element_type=F32).astype(BF16)
        mine_out[...] = answer[:half]
        other_out[...] = answer[half:]


def expert_share(mine, other, up_rows, down_rows, *earlier):
    half, features = mine.shape
    units = up_rows.shape[0]
    steps = 4
    chunk, width = units // steps, features // steps
    shape = jax.ShapeDtypeStruct((half, features), BF16)
    whole = pl.BlockSpec((half, features), lambda i: (0, 0))
    part = pl.BlockSpec((half, width), lambda i: (0, jnp.maximum(i - steps, 0)))
    return pl.pallas_call(
        functools.partial(expert_kernel, steps, half),
        grid=(2 * steps,),
        out_shape=[shape] * 2,
        in_specs=[
            whole,
            whole,
            pl.BlockSpec((chunk, features), lambda i: (jnp.minimum(i, steps - 1), 0)),
            pl.BlockSpec((units, width), lambda i: (0, jnp.maximum(i - steps, 0))),
            *[pl.BlockSpec(memory_space=pl.ANY) for _ in earlier],
        ],
        out_specs=[part] * 2,
        scratch_shapes=[pltpu.VMEM((2 * half, features), BF16), pltpu.VMEM((2 * half, units), BF16)],
        cost_estimate=pl.CostEstimate(
            flops=8 * half * units * features,
            bytes_accessed=4 * units * features + 8 * half * features,
            transcendentals=2 * half * units,
        ),
        compiler_params=pltpu.CompilerParams(vmem_limit_bytes=40 * 2**20),
    )(mine, other, up_rows, down_rows, *earlier)


def pack_kernel(count, half, pick_ref, *refs):
    mine_ref, other_ref, group = refs[-3:]
    tok_rows, at = refs[0].shape[-2], 0
    for block in refs[:count]:
        rows = block.shape[-2]
        group[at : at + rows] = block[...].reshape(rows, block.shape[-1])
        at += rows
    chosen = jnp.dot(pick_ref[0], group[...], preferred_element_type=F32).astype(BF16)
    mine_ref[...] = chosen[:half]
    other_ref[...] = chosen[half:]


def pack(m, pick, blocks, *earlier):
    _, rows, tokens = pick.shape
    half, features = rows // 2, blocks[0].shape[-1]
    width = features // 4

    def spec(block):
        if block.ndim == 3:
            return pl.BlockSpec((1, block.shape[1], width), lambda i: (m, 0, i))
        return pl.BlockSpec((block.shape[0], width), lambda i: (0, i))

    return pl.pallas_call(
        functools.partial(pack_kernel, len(blocks), half),
        grid=(features // width,),
        out_shape=[jax.ShapeDtypeStruct((half, features), BF16)] * 2,
        in_specs=[
            pl.BlockSpec((1, rows, tokens), lambda i: (m, 0, 0)),
            *[spec(block) for block in blocks],
            *[pl.BlockSpec(memory_space=pl.ANY) for _ in earlier],
        ],
        out_specs=[pl.BlockSpec((half, width), lambda i: (0, i))] * 2,
        scratch_shapes=[pltpu.VMEM((tokens, width), BF16)],
        cost_estimate=pl.CostEstimate(
            flops=2 * rows * tokens * features,
            bytes_accessed=2 * (rows + tokens) * features + 2 * rows * tokens,
            transcendentals=0,
        ),
        compiler_params=pltpu.CompilerParams(vmem_limit_bytes=24 * 2**20),
    )(pick, *blocks, *earlier)


def unpack_kernel(stays, skipped, mine_ref, other_ref, high_ref, low_ref, *refs):
    refs, answers = refs[skipped:], refs[-1]
    half = mine_ref.shape[0]
    answers[:half] = mine_ref[...]
    answers[half:] = other_ref[...]
    total = None
    for part in (high_ref, low_ref):
        term = jnp.dot(part[0], answers[...], preferred_element_type=F32)
        total = term if total is None else total + term
    refs[0][...] = total[:stays]
    for n, out in enumerate(refs[1:-1]):
        out[...] = total[(n + 1) * stays : (n + 2) * stays].astype(BF16)


def unpack(m, sides, mine, other, high, low, *earlier):
    _, tokens, rows = high.shape
    half, features = mine.shape
    width, stays = features // 4, tokens // sides
    out_shape = [jax.ShapeDtypeStruct((stays, features), F32)]
    out_shape += [jax.ShapeDtypeStruct((stays, features), BF16)] * (sides - 1)
    part = pl.BlockSpec((half, width), lambda i: (0, i))
    whole = pl.BlockSpec((1, tokens, rows), lambda i: (m, 0, 0))
    return pl.pallas_call(
        functools.partial(unpack_kernel, stays, len(earlier)),
        grid=(features // width,),
        out_shape=out_shape,
        in_specs=[part, part, whole, whole, *[pl.BlockSpec(memory_space=pl.ANY) for _ in earlier]],
        out_specs=[pl.BlockSpec((shape.shape[0], width), lambda i: (0, i)) for shape in out_shape],
        scratch_shapes=[pltpu.VMEM((rows, width), BF16)],
        cost_estimate=pl.CostEstimate(
            flops=4 * rows * tokens * features,
            bytes_accessed=2 * (rows + 2 * tokens) * features + 4 * rows * tokens,
            transcendentals=0,
        ),
        compiler_params=pltpu.CompilerParams(vmem_limit_bytes=24 * 2**20),
    )(mine, other, high, low, *earlier)


def after(value, *earlier):
    return lax.optimization_barrier((value,) + earlier)[0] if earlier else value


def on_device(tokens, routes, combine, expert_home, up_weight, down_weight):
    up_rows = up_weight[0, 0]
    down_rows = down_weight[0, 0]
    batches, tok_rows, features = tokens.shape
    top_count = routes.shape[2]
    experts = expert_home.shape[0]
    sides = lax.axis_size("expert") // 2
    capacity = min(tok_rows, tok_rows * top_count // experts + tok_rows // 32)
    here = lax.axis_index("expert")
    place = jnp.stack([here // 2, here % 2]).astype(jnp.int32)
    half = -(-sides * 4 * capacity // 16) * 16

    facts = []
    for m in range(batches):
        home, rank = placed_pairs(routes[m], expert_home)
        facts += [(home * tok_rows + rank).astype(F32), combine[m].T]
    facts = jnp.concatenate(facts)
    facts = jnp.stack([facts] + [swapped(facts, "dp", bits) for bits in (1, 2, 3)])

    def across(block):
        return [swapped(block, "expert", 2 * j) for j in range(1, sides)]

    own_x = across(tokens)
    far, both = [None] * batches, [None] * batches
    pair, pair_x, both_x = [None], [None], [None]
    near = swapped(after(tokens, facts), "dp", 1)
    far[0] = swapped(after(tokens[0], facts), "dp", 2)
    facts_x = jnp.stack([facts] + across(facts))
    pick, high, low = plan(place, facts_x, batches, top_count, capacity, half)
    both[0] = swapped(far[0], "dp", 1)
    pair[0] = jnp.concatenate([near[0], far[0]])
    pair_x[0] = across(after(pair[0], facts_x))
    far[1] = swapped(after(tokens[1], far[0]), "dp", 2)
    both_x[0] = across(both[0])
    both[1] = swapped(far[1], "dp", 1)
    triple = jnp.concatenate([near[1], far[1], both[1]])
    triple_x = across(triple)

    def packed(m, blocks, *earlier):
        mine, other = pack(m, pick, [tokens] + own_x + blocks, *earlier)
        return mine, swapped(other, "expert", 1)

    def crossed(block):
        part = block.shape[0] // 48 * 16
        cuts = [block[at : at + part] for at in range(0, block.shape[0], part)]
        return jnp.concatenate([swapped(cut, "expert", 1) for cut in cuts])

    def unpacked(m, mine, other, *earlier):
        return unpack(m, sides, mine, crossed(other), high, low, *earlier)

    def near_sum(staying, first):
        return sum([block.astype(F32) for block in first], staying[: 2 * tok_rows]).astype(BF16)

    def far_sums(staying, second, back):
        return sum([block.astype(F32) for block in second + [back]], staying[2 * tok_rows :])

    rows_0 = packed(0, [pair[0]] + pair_x[0] + [both[0]] + both_x[0], triple)
    answers_0 = expert_share(*rows_0, up_rows, down_rows)
    rows_1 = packed(1, [triple] + triple_x, answers_0[0])
    staying_0, *leaving_0 = unpacked(0, *answers_0, *triple_x)
    sums_0 = [swapped(block, "expert", 2 * j + 2) for j, block in enumerate(leaving_0)]
    answers_1 = expert_share(*rows_1, up_rows, down_rows, leaving_0[0])
    staying_1, *leaving_1 = unpacked(1, *answers_1, *sums_0)
    count = 2 * tok_rows
    first_1, second_1 = (
        [swapped(block[at : at + count], "expert", 2 * j + 2) for j, block in enumerate(leaving_1)]
        for at in (0, count)
    )
    back_0 = swapped(near_sum(staying_0, [b[:count] for b in sums_0]), "dp", 1)
    total_0 = far_sums(staying_0, [b[count:] for b in sums_0], back_0)
    far_0 = swapped(total_0[:tok_rows].astype(BF16), "dp", 2)
    back_1 = swapped(after(near_sum(staying_1, first_1), back_0), "dp", 1)
    total_1 = far_sums(staying_1, second_1, back_1)
    far_1 = swapped(after(total_1[:tok_rows].astype(BF16), far_0), "dp", 2)
    totals = [
        passed_along((total[tok_rows:] + far_part.astype(F32)).astype(BF16), "segment", 1)
        for total, far_part in ((total_0, far_0), (total_1, far_1))
    ]
    return jnp.stack(totals, axis=0)


def solution(mesh):
    return jax.shard_map(
        on_device,
        mesh=mesh,
        in_specs=(
            P(None, ("segment", "expert", "dp"), None),
            P(None, ("segment", "expert", "dp"), None),
            P(None, ("segment", "expert", "dp"), None),
            P(),
            P("segment", "expert", "dp", None),
            P("segment", "expert", "dp", None),
        ),
        out_specs=P(None, ("segment", "expert", "dp"), None),
        check_vma=False,
    )
```

```python
import functools

import jax
import jax.numpy as jnp
from jax import lax
from jax.experimental import pallas as pl
from jax.experimental.pallas import tpu as pltpu
from jax.sharding import PartitionSpec as P

BF16, F32 = jnp.bfloat16, jnp.float32


def passed_along(block, axis, distance):
    devices = range(lax.axis_size(axis))
    route = [((i - distance) % len(devices), i) for i in devices]
    return lax.ppermute(block, axis, route)


def swapped(block, axis, bits):
    return lax.ppermute(block, axis, [(i, i ^ bits) for i in range(lax.axis_size(axis))])


def placed_pairs(routes, expert_home):
    first, second = routes[:, 0], routes[:, 1]
    count = routes.shape[0]
    earlier = jnp.arange(count)[:, None] < jnp.arange(count)[None, :]
    rank_first = jnp.sum(jnp.where(earlier & (first[:, None] == first[None, :]), 1, 0), axis=0)
    rank_second = jnp.sum(
        jnp.where(first[:, None] == second[None, :], 1, 0)
        + jnp.where(earlier & (second[:, None] == second[None, :]), 1, 0),
        axis=0,
    )
    chosen = routes.T
    ids = jnp.arange(expert_home.shape[0], dtype=jnp.int32)
    home = jnp.sum(jnp.where(chosen[:, :, None] == ids, expert_home, 0), axis=-1)
    return home, jnp.stack([rank_first, rank_second])


def arrivals(sides, batch):
    steps = ((0,), (1, 2), (3,)) if batch == 0 else ((0,), (1, 2, 3))
    return [(j, bits) for step in steps for j in range(sides) for bits in step]


def departures(sides, batch):
    order = (3, 1, 2, 0) if batch == 0 else (3, 2, 1, 0)
    return [(j, bits) for j in range(sides) for bits in order]


def plan_kernel(sides, batches, top_count, capacity, half, place_ref, facts_ref, pick_ref, high_ref, low_ref):
    side, core = place_ref[0], place_ref[1]
    tok_rows = facts_ref.shape[-1]
    rows = 2 * half
    tokens = sides * 4 * tok_rows
    padded = -(-rows // 128) * 128
    ids = lax.broadcasted_iota(jnp.int32, (padded, tokens), 0)
    for m in range(batches):
        pick = jnp.zeros((rows, tokens), F32)
        mix = jnp.zeros((padded, tokens), F32)
        for k in range(top_count):
            slots, weights = {}, {}
            for j, bits in departures(sides, m):
                at = m * 2 * top_count + k
                code = facts_ref[j, bits, at : at + 1, :].astype(jnp.int32)
                at = at + top_count
                weights[j, bits] = facts_ref[j, bits, at : at + 1, :]
                home, rank = code // tok_rows, code % tok_rows
                slot = (j * 4 + bits) * capacity + rank + jnp.where(home % 2 == core, 0, half)
                slots[j, bits] = jnp.where(home // 2 == side, slot, -1)
            hit = ids[:rows] == jnp.concatenate([slots[at] for at in arrivals(sides, m)], axis=1)
            pick = jnp.where(hit, 1.0, pick)
            hit = ids == jnp.concatenate([slots[at] for at in departures(sides, m)], axis=1)
            mix = jnp.where(hit, jnp.concatenate([weights[at] for at in departures(sides, m)], axis=1), mix)
        mix = mix.T[:, :rows]
        high = mix.astype(BF16)
        pick_ref[m] = pick.astype(BF16)
        high_ref[m] = high
        low_ref[m] = (mix - high.astype(F32)).astype(BF16)


def plan(place, facts, batches, top_count, capacity, half):
    sides, tok_rows = facts.shape[0], facts.shape[-1]
    shape = jax.ShapeDtypeStruct((batches, 2 * half, sides * 4 * tok_rows), BF16)
    mixed = jax.ShapeDtypeStruct((batches, sides * 4 * tok_rows, 2 * half), BF16)
    vmem = pl.BlockSpec(memory_space=pltpu.VMEM)
    return pl.pallas_call(
        functools.partial(plan_kernel, sides, batches, top_count, capacity, half),
        out_shape=[shape, mixed, mixed],
        in_specs=[pl.BlockSpec(memory_space=pltpu.SMEM), vmem],
        out_specs=[vmem] * 3,
        cost_estimate=pl.CostEstimate(
            flops=10 * shape.size, bytes_accessed=6 * shape.size, transcendentals=0
        ),
        compiler_params=pltpu.CompilerParams(vmem_limit_bytes=32 * 2**20),
    )(place, facts)


def expert_kernel(steps, half, mine_ref, other_ref, up_ref, down_ref, *refs):
    mine_out, other_out, rows, hidden = refs[-4:]
    step = pl.program_id(0)
    chunk = up_ref.shape[0]

    @pl.when(step == 0)
    def _():
        rows[:half] = mine_ref[...]
        rows[half:] = other_ref[...]

    for s in range(steps):

        @pl.when(step == s)
        def _():
            pre_act = lax.dot_general(
                rows[...], up_ref[...], (((1,), (1,)), ((), ())), preferred_element_type=F32
            )
            hidden[:, s * chunk : (s + 1) * chunk] = jax.nn.silu(pre_act).astype(BF16)

    @pl.when(step >= steps)
    def _():
        answer = jnp.dot(hidden[...], down_ref[...], preferred_element_type=F32).astype(BF16)
        mine_out[...] = answer[:half]
        other_out[...] = answer[half:]


def expert_share(mine, other, up_rows, down_rows, *earlier):
    half, features = mine.shape
    units = up_rows.shape[0]
    steps = 4
    chunk, width = units // steps, features // steps
    shape = jax.ShapeDtypeStruct((half, features), BF16)
    whole = pl.BlockSpec((half, features), lambda i: (0, 0))
    part = pl.BlockSpec((half, width), lambda i: (0, jnp.maximum(i - steps, 0)))
    return pl.pallas_call(
        functools.partial(expert_kernel, steps, half),
        grid=(2 * steps,),
        out_shape=[shape] * 2,
        in_specs=[
            whole,
            whole,
            pl.BlockSpec((chunk, features), lambda i: (jnp.minimum(i, steps - 1), 0)),
            pl.BlockSpec((units, width), lambda i: (0, jnp.maximum(i - steps, 0))),
            *[pl.BlockSpec(memory_space=pl.ANY) for _ in earlier],
        ],
        out_specs=[part] * 2,
        scratch_shapes=[pltpu.VMEM((2 * half, features), BF16), pltpu.VMEM((2 * half, units), BF16)],
        cost_estimate=pl.CostEstimate(
            flops=8 * half * units * features,
            bytes_accessed=4 * units * features + 8 * half * features,
            transcendentals=2 * half * units,
        ),
        compiler_params=pltpu.CompilerParams(vmem_limit_bytes=40 * 2**20),
    )(mine, other, up_rows, down_rows, *earlier)


def pack_kernel(count, half, pick_ref, *refs):
    mine_ref, other_ref, group = refs[-3:]
    tok_rows, at = refs[0].shape[-2], 0
    for block in refs[:count]:
        rows = block.shape[-2]
        group[at : at + rows] = block[...].reshape(rows, block.shape[-1])
        at += rows
    chosen = jnp.dot(pick_ref[0], group[...], preferred_element_type=F32).astype(BF16)
    mine_ref[...] = chosen[:half]
    other_ref[...] = chosen[half:]


def pack(m, pick, blocks, *earlier):
    _, rows, tokens = pick.shape
    half, features = rows // 2, blocks[0].shape[-1]
    width = features // 4

    def spec(block):
        if block.ndim == 3:
            return pl.BlockSpec((1, block.shape[1], width), lambda i: (m, 0, i))
        return pl.BlockSpec((block.shape[0], width), lambda i: (0, i))

    return pl.pallas_call(
        functools.partial(pack_kernel, len(blocks), half),
        grid=(features // width,),
        out_shape=[jax.ShapeDtypeStruct((half, features), BF16)] * 2,
        in_specs=[
            pl.BlockSpec((1, rows, tokens), lambda i: (m, 0, 0)),
            *[spec(block) for block in blocks],
            *[pl.BlockSpec(memory_space=pl.ANY) for _ in earlier],
        ],
        out_specs=[pl.BlockSpec((half, width), lambda i: (0, i))] * 2,
        scratch_shapes=[pltpu.VMEM((tokens, width), BF16)],
        cost_estimate=pl.CostEstimate(
            flops=2 * rows * tokens * features,
            bytes_accessed=2 * (rows + tokens) * features + 2 * rows * tokens,
            transcendentals=0,
        ),
        compiler_params=pltpu.CompilerParams(vmem_limit_bytes=24 * 2**20),
    )(pick, *blocks, *earlier)


def unpack_kernel(stays, skipped, mine_ref, other_ref, high_ref, low_ref, *refs):
    refs, answers = refs[skipped:], refs[-1]
    half = mine_ref.shape[0]
    answers[:half] = mine_ref[...]
    answers[half:] = other_ref[...]
    total = None
    for part in (high_ref, low_ref):
        term = jnp.dot(part[0], answers[...], preferred_element_type=F32)
        total = term if total is None else total + term
    refs[0][...] = total[:stays]
    for n, out in enumerate(refs[1:-1]):
        out[...] = total[(n + 1) * stays : (n + 2) * stays].astype(BF16)


def unpack(m, sides, mine, other, high, low, *earlier):
    _, tokens, rows = high.shape
    half, features = mine.shape
    width, stays = features // 4, tokens // sides
    out_shape = [jax.ShapeDtypeStruct((stays, features), F32)]
    out_shape += [jax.ShapeDtypeStruct((stays, features), BF16)] * (sides - 1)
    part = pl.BlockSpec((half, width), lambda i: (0, i))
    whole = pl.BlockSpec((1, tokens, rows), lambda i: (m, 0, 0))
    return pl.pallas_call(
        functools.partial(unpack_kernel, stays, len(earlier)),
        grid=(features // width,),
        out_shape=out_shape,
        in_specs=[part, part, whole, whole, *[pl.BlockSpec(memory_space=pl.ANY) for _ in earlier]],
        out_specs=[pl.BlockSpec((shape.shape[0], width), lambda i: (0, i)) for shape in out_shape],
        scratch_shapes=[pltpu.VMEM((rows, width), BF16)],
        cost_estimate=pl.CostEstimate(
            flops=4 * rows * tokens * features,
            bytes_accessed=2 * (rows + 2 * tokens) * features + 4 * rows * tokens,
            transcendentals=0,
        ),
        compiler_params=pltpu.CompilerParams(vmem_limit_bytes=24 * 2**20),
    )(mine, other, high, low, *earlier)


def after(value, *earlier):
    return lax.optimization_barrier((value,) + earlier)[0] if earlier else value


def on_device(tokens, routes, combine, expert_home, up_weight, down_weight):
    up_rows = up_weight[0, 0]
    down_rows = down_weight[0, 0]
    batches, tok_rows, features = tokens.shape
    top_count = routes.shape[2]
    experts = expert_home.shape[0]
    sides = lax.axis_size("expert") // 2
    capacity = min(tok_rows, tok_rows * top_count // experts + tok_rows // 32)
    here = lax.axis_index("expert")
    place = jnp.stack([here // 2, here % 2]).astype(jnp.int32)
    half = -(-sides * 4 * capacity // 16) * 16

    facts = []
    for m in range(batches):
        home, rank = placed_pairs(routes[m], expert_home)
        facts += [(home * tok_rows + rank).astype(F32), combine[m].T]
    facts = jnp.concatenate(facts)
    facts = jnp.stack([facts] + [swapped(facts, "dp", bits) for bits in (1, 2, 3)])

    def across(block):
        return [swapped(block, "expert", 2 * j) for j in range(1, sides)]

    own_x = across(tokens)
    far, both = [None] * batches, [None] * batches
    pair, pair_x, both_x = [None], [None], [None]
    near = swapped(after(tokens, facts), "dp", 1)
    far[0] = swapped(after(tokens[0], facts), "dp", 2)
    facts_x = jnp.stack([facts] + across(facts))
    pick, high, low = plan(place, facts_x, batches, top_count, capacity, half)
    both[0] = swapped(far[0], "dp", 1)
    pair[0] = jnp.concatenate([near[0], far[0]])
    pair_x[0] = across(after(pair[0], facts_x))
    far[1] = swapped(after(tokens[1], far[0]), "dp", 2)
    both_x[0] = across(both[0])
    both[1] = swapped(far[1], "dp", 1)
    triple = jnp.concatenate([near[1], far[1], both[1]])
    triple_x = across(triple)

    def packed(m, blocks, *earlier):
        mine, other = pack(m, pick, [tokens] + own_x + blocks, *earlier)
        return mine, swapped(other, "expert", 1)

    def crossed(block):
        part = block.shape[0] // 48 * 16
        cuts = [block[at : at + part] for at in range(0, block.shape[0], part)]
        return jnp.concatenate([swapped(cut, "expert", 1) for cut in cuts])

    def unpacked(m, mine, other, *earlier):
        return unpack(m, sides, mine, other, high, low, *earlier)

    def near_sum(staying, first):
        return sum([block.astype(F32) for block in first], staying[: 2 * tok_rows]).astype(BF16)

    def far_sums(staying, second, back):
        return sum([block.astype(F32) for block in second + [back]], staying[2 * tok_rows :])

    rows_0 = packed(0, [pair[0]] + pair_x[0] + [both[0]] + both_x[0], triple)
    answers_0 = expert_share(*rows_0, up_rows, down_rows)
    rows_1 = packed(1, [triple] + triple_x, answers_0[0])
    other = swapped(after(answers_0[1], *triple_x), "expert", 1)
    staying_0, *leaving_0 = unpacked(0, answers_0[0], other)
    sums_0 = [swapped(block, "expert", 2 * j + 2) for j, block in enumerate(leaving_0)]
    answers_1 = expert_share(*rows_1, up_rows, down_rows, leaving_0[0])
    staying_1, *leaving_1 = unpacked(1, answers_1[0], crossed(answers_1[1]))
    count = 2 * tok_rows
    leaving_1 = [after(block, *sums_0) for block in leaving_1]
    far_1, pair_1 = (
        [swapped(block[at : at + tok_rows], "expert", 2 * j + 2) for j, block in enumerate(leaving_1)]
        for at in (0, tok_rows)
    )
    back_0 = swapped(near_sum(staying_0, [b[:count] for b in sums_0]), "dp", 1)
    total_0 = far_sums(staying_0, [b[count:] for b in sums_0], back_0)
    far_0 = swapped(total_0[:tok_rows].astype(BF16), "dp", 2)
    def summed(at, blocks):
        return sum([block.astype(F32) for block in blocks], staying_1[at * tok_rows : (at + 1) * tok_rows])

    back_1 = swapped(summed(0, far_1).astype(BF16), "dp", 1)
    rest_1 = [
        swapped(after(block[count:], back_1, *pair_1), "expert", 2 * j + 2) for j, block in enumerate(leaving_1)
    ]
    total_1 = summed(1, pair_1 + [back_1])
    far_1 = swapped(total_1.astype(BF16), "dp", 2)
    back = swapped(summed(2, [block[:tok_rows] for block in rest_1]).astype(BF16), "dp", 1)
    total_1 = summed(3, [block[tok_rows:] for block in rest_1] + [back, far_1])
    total_0 = total_0[tok_rows:] + far_0.astype(F32)
    totals = [passed_along(total.astype(BF16), "segment", 1) for total in (total_0, total_1)]
    return jnp.stack(totals, axis=0)


def solution(mesh):
    return jax.shard_map(
        on_device,
        mesh=mesh,
        in_specs=(
            P(None, ("segment", "expert", "dp"), None),
            P(None, ("segment", "expert", "dp"), None),
            P(None, ("segment", "expert", "dp"), None),
            P(),
            P("segment", "expert", "dp", None),
            P("segment", "expert", "dp", None),
        ),
        out_specs=P(None, ("segment", "expert", "dp"), None),
        check_vma=False,
    )
```

```python
import functools

import jax
import jax.numpy as jnp
from jax import lax
from jax.experimental import pallas as pl
from jax.experimental.pallas import tpu as pltpu
from jax.sharding import PartitionSpec as P

BF16, F32 = jnp.bfloat16, jnp.float32


def passed_along(block, axis, distance):
    devices = range(lax.axis_size(axis))
    route = [((i - distance) % len(devices), i) for i in devices]
    return lax.ppermute(block, axis, route)


def swapped(block, axis, bits):
    return lax.ppermute(block, axis, [(i, i ^ bits) for i in range(lax.axis_size(axis))])


def placed_pairs(routes, expert_home):
    first, second = routes[:, 0], routes[:, 1]
    count = routes.shape[0]
    earlier = jnp.arange(count)[:, None] < jnp.arange(count)[None, :]
    rank_first = jnp.sum(jnp.where(earlier & (first[:, None] == first[None, :]), 1, 0), axis=0)
    rank_second = jnp.sum(
        jnp.where(first[:, None] == second[None, :], 1, 0)
        + jnp.where(earlier & (second[:, None] == second[None, :]), 1, 0),
        axis=0,
    )
    chosen = routes.T
    ids = jnp.arange(expert_home.shape[0], dtype=jnp.int32)
    home = jnp.sum(jnp.where(chosen[:, :, None] == ids, expert_home, 0), axis=-1)
    return home, jnp.stack([rank_first, rank_second])


def arrivals(sides, batch):
    steps = ((0,), (1, 2), (3,)) if batch == 0 else ((0,), (1, 2, 3))
    return [(j, bits) for step in steps for j in range(sides) for bits in step]


def departures(sides, batch):
    order = (3, 1, 2, 0) if batch == 0 else (3, 2, 1, 0)
    return [(j, bits) for j in range(sides) for bits in order]


def plan_kernel(sides, batches, top_count, capacity, half, place_ref, facts_ref, pick_ref, high_ref, low_ref):
    side, core = place_ref[0], place_ref[1]
    tok_rows = facts_ref.shape[-1]
    rows = 2 * half
    tokens = sides * 4 * tok_rows
    padded = -(-rows // 128) * 128
    ids = lax.broadcasted_iota(jnp.int32, (padded, tokens), 0)
    for m in range(batches):
        pick = jnp.zeros((rows, tokens), F32)
        mix = jnp.zeros((padded, tokens), F32)
        for k in range(top_count):
            slots, weights = {}, {}
            for j, bits in departures(sides, m):
                at = m * 2 * top_count + k
                code = facts_ref[j, bits, at : at + 1, :].astype(jnp.int32)
                at = at + top_count
                weights[j, bits] = facts_ref[j, bits, at : at + 1, :]
                home, rank = code // tok_rows, code % tok_rows
                slot = (j * 4 + bits) * capacity + rank + jnp.where(home % 2 == core, 0, half)
                slots[j, bits] = jnp.where(home // 2 == side, slot, -1)
            hit = ids[:rows] == jnp.concatenate([slots[at] for at in arrivals(sides, m)], axis=1)
            pick = jnp.where(hit, 1.0, pick)
            hit = ids == jnp.concatenate([slots[at] for at in departures(sides, m)], axis=1)
            mix = jnp.where(hit, jnp.concatenate([weights[at] for at in departures(sides, m)], axis=1), mix)
        mix = mix.T[:, :rows]
        high = mix.astype(BF16)
        pick_ref[m] = pick.astype(BF16)
        high_ref[m] = high
        low_ref[m] = (mix - high.astype(F32)).astype(BF16)


def plan(place, facts, batches, top_count, capacity, half):
    sides, tok_rows = facts.shape[0], facts.shape[-1]
    shape = jax.ShapeDtypeStruct((batches, 2 * half, sides * 4 * tok_rows), BF16)
    mixed = jax.ShapeDtypeStruct((batches, sides * 4 * tok_rows, 2 * half), BF16)
    vmem = pl.BlockSpec(memory_space=pltpu.VMEM)
    return pl.pallas_call(
        functools.partial(plan_kernel, sides, batches, top_count, capacity, half),
        out_shape=[shape, mixed, mixed],
        in_specs=[pl.BlockSpec(memory_space=pltpu.SMEM), vmem],
        out_specs=[vmem] * 3,
        cost_estimate=pl.CostEstimate(
            flops=10 * shape.size, bytes_accessed=6 * shape.size, transcendentals=0
        ),
        compiler_params=pltpu.CompilerParams(vmem_limit_bytes=32 * 2**20),
    )(place, facts)


def expert_kernel(steps, half, mine_ref, other_ref, up_ref, down_ref, *refs):
    mine_out, other_out, rows, hidden = refs[-4:]
    step = pl.program_id(0)
    chunk = up_ref.shape[0]

    @pl.when(step == 0)
    def _():
        rows[:half] = mine_ref[...]
        rows[half:] = other_ref[...]

    for s in range(steps):

        @pl.when(step == s)
        def _():
            pre_act = lax.dot_general(
                rows[...], up_ref[...], (((1,), (1,)), ((), ())), preferred_element_type=F32
            )
            hidden[:, s * chunk : (s + 1) * chunk] = jax.nn.silu(pre_act).astype(BF16)

    @pl.when(step >= steps)
    def _():
        answer = jnp.dot(hidden[...], down_ref[...], preferred_element_type=F32).astype(BF16)
        mine_out[...] = answer[:half]
        other_out[...] = answer[half:]


def expert_share(mine, other, up_rows, down_rows, *earlier):
    half, features = mine.shape
    units = up_rows.shape[0]
    steps = 2
    chunk, width = units // steps, features // steps
    shape = jax.ShapeDtypeStruct((half, features), BF16)
    whole = pl.BlockSpec((half, features), lambda i: (0, 0))
    part = pl.BlockSpec((half, width), lambda i: (0, jnp.maximum(i - steps, 0)))
    return pl.pallas_call(
        functools.partial(expert_kernel, steps, half),
        grid=(2 * steps,),
        out_shape=[shape] * 2,
        in_specs=[
            whole,
            whole,
            pl.BlockSpec((chunk, features), lambda i: (jnp.minimum(i, steps - 1), 0)),
            pl.BlockSpec((units, width), lambda i: (0, jnp.maximum(i - steps, 0))),
            *[pl.BlockSpec(memory_space=pl.ANY) for _ in earlier],
        ],
        out_specs=[part] * 2,
        scratch_shapes=[pltpu.VMEM((2 * half, features), BF16), pltpu.VMEM((2 * half, units), BF16)],
        cost_estimate=pl.CostEstimate(
            flops=8 * half * units * features,
            bytes_accessed=4 * units * features + 8 * half * features,
            transcendentals=2 * half * units,
        ),
        compiler_params=pltpu.CompilerParams(vmem_limit_bytes=52 * 2**20),
    )(mine, other, up_rows, down_rows, *earlier)


def pack_kernel(count, half, pick_ref, *refs):
    mine_ref, other_ref, group = refs[-3:]
    tok_rows, at = refs[0].shape[-2], 0
    for block in refs[:count]:
        rows = block.shape[-2]
        group[at : at + rows] = block[...].reshape(rows, block.shape[-1])
        at += rows
    chosen = jnp.dot(pick_ref[0], group[...], preferred_element_type=F32).astype(BF16)
    mine_ref[...] = chosen[:half]
    other_ref[...] = chosen[half:]


def pack(m, pick, blocks, *earlier):
    _, rows, tokens = pick.shape
    half, features = rows // 2, blocks[0].shape[-1]
    width = features // 4

    def spec(block):
        if block.ndim == 3:
            return pl.BlockSpec((1, block.shape[1], width), lambda i: (m, 0, i))
        return pl.BlockSpec((block.shape[0], width), lambda i: (0, i))

    return pl.pallas_call(
        functools.partial(pack_kernel, len(blocks), half),
        grid=(features // width,),
        out_shape=[jax.ShapeDtypeStruct((half, features), BF16)] * 2,
        in_specs=[
            pl.BlockSpec((1, rows, tokens), lambda i: (m, 0, 0)),
            *[spec(block) for block in blocks],
            *[pl.BlockSpec(memory_space=pl.ANY) for _ in earlier],
        ],
        out_specs=[pl.BlockSpec((half, width), lambda i: (0, i))] * 2,
        scratch_shapes=[pltpu.VMEM((tokens, width), BF16)],
        cost_estimate=pl.CostEstimate(
            flops=2 * rows * tokens * features,
            bytes_accessed=2 * (rows + tokens) * features + 2 * rows * tokens,
            transcendentals=0,
        ),
        compiler_params=pltpu.CompilerParams(vmem_limit_bytes=24 * 2**20),
    )(pick, *blocks, *earlier)


def unpack_kernel(stays, skipped, mine_ref, other_ref, high_ref, low_ref, *refs):
    refs, answers = refs[skipped:], refs[-1]
    half = mine_ref.shape[0]
    answers[:half] = mine_ref[...]
    answers[half:] = other_ref[...]
    total = None
    for part in (high_ref, low_ref):
        term = jnp.dot(part[0], answers[...], preferred_element_type=F32)
        total = term if total is None else total + term
    refs[0][...] = total[:stays]
    for n, out in enumerate(refs[1:-1]):
        out[...] = total[(n + 1) * stays : (n + 2) * stays].astype(BF16)


def unpack(m, sides, mine, other, high, low, *earlier):
    _, tokens, rows = high.shape
    half, features = mine.shape
    width, stays = features // 4, tokens // sides
    out_shape = [jax.ShapeDtypeStruct((stays, features), F32)]
    out_shape += [jax.ShapeDtypeStruct((stays, features), BF16)] * (sides - 1)
    part = pl.BlockSpec((half, width), lambda i: (0, i))
    whole = pl.BlockSpec((1, tokens, rows), lambda i: (m, 0, 0))
    return pl.pallas_call(
        functools.partial(unpack_kernel, stays, len(earlier)),
        grid=(features // width,),
        out_shape=out_shape,
        in_specs=[part, part, whole, whole, *[pl.BlockSpec(memory_space=pl.ANY) for _ in earlier]],
        out_specs=[pl.BlockSpec((shape.shape[0], width), lambda i: (0, i)) for shape in out_shape],
        scratch_shapes=[pltpu.VMEM((rows, width), BF16)],
        cost_estimate=pl.CostEstimate(
            flops=4 * rows * tokens * features,
            bytes_accessed=2 * (rows + 2 * tokens) * features + 4 * rows * tokens,
            transcendentals=0,
        ),
        compiler_params=pltpu.CompilerParams(vmem_limit_bytes=24 * 2**20),
    )(mine, other, high, low, *earlier)


def after(value, *earlier):
    return lax.optimization_barrier((value,) + earlier)[0] if earlier else value


def on_device(tokens, routes, combine, expert_home, up_weight, down_weight):
    up_rows = up_weight[0, 0]
    down_rows = down_weight[0, 0]
    batches, tok_rows, features = tokens.shape
    top_count = routes.shape[2]
    experts = expert_home.shape[0]
    sides = lax.axis_size("expert") // 2
    capacity = min(tok_rows, tok_rows * top_count // experts + tok_rows // 32)
    here = lax.axis_index("expert")
    place = jnp.stack([here // 2, here % 2]).astype(jnp.int32)
    half = -(-sides * 4 * capacity // 16) * 16

    facts = []
    for m in range(batches):
        home, rank = placed_pairs(routes[m], expert_home)
        facts += [(home * tok_rows + rank).astype(F32), combine[m].T]
    facts = jnp.concatenate(facts)
    facts = jnp.stack([facts] + [swapped(facts, "dp", bits) for bits in (1, 2, 3)])

    def across(block):
        return [swapped(block, "expert", 2 * j) for j in range(1, sides)]

    own_x = across(tokens)
    far, both = [None] * batches, [None] * batches
    pair, pair_x, both_x = [None], [None], [None]
    near = swapped(after(tokens, facts), "dp", 1)
    far[0] = swapped(after(tokens[0], facts), "dp", 2)
    facts_x = jnp.stack([facts] + across(facts))
    pick, high, low = plan(place, facts_x, batches, top_count, capacity, half)
    both[0] = swapped(far[0], "dp", 1)
    pair[0] = jnp.concatenate([near[0], far[0]])
    pair_x[0] = across(after(pair[0], facts_x))
    far[1] = swapped(after(tokens[1], far[0]), "dp", 2)
    both_x[0] = across(both[0])
    both[1] = swapped(far[1], "dp", 1)
    triple = jnp.concatenate([near[1], far[1], both[1]])
    triple_x = across(triple)

    def packed(m, blocks, *earlier):
        mine, other = pack(m, pick, [tokens] + own_x + blocks, *earlier)
        return mine, swapped(other, "expert", 1)

    def crossed(block):
        part = block.shape[0] // 48 * 16
        cuts = [block[at : at + part] for at in range(0, block.shape[0], part)]
        return jnp.concatenate([swapped(cut, "expert", 1) for cut in cuts])

    def unpacked(m, mine, other, *earlier):
        return unpack(m, sides, mine, other, high, low, *earlier)

    def near_sum(staying, first):
        return sum([block.astype(F32) for block in first], staying[: 2 * tok_rows]).astype(BF16)

    def far_sums(staying, second, back):
        return sum([block.astype(F32) for block in second + [back]], staying[2 * tok_rows :])

    rows_0 = packed(0, [pair[0]] + pair_x[0] + [both[0]] + both_x[0], triple)
    answers_0 = expert_share(*rows_0, up_rows, down_rows)
    rows_1 = packed(1, [triple] + triple_x, answers_0[0])
    other = swapped(after(answers_0[1], *triple_x), "expert", 1)
    staying_0, *leaving_0 = unpacked(0, answers_0[0], other)
    sums_0 = [swapped(block, "expert", 2 * j + 2) for j, block in enumerate(leaving_0)]
    answers_1 = expert_share(*rows_1, up_rows, down_rows, leaving_0[0])
    staying_1, *leaving_1 = unpacked(1, answers_1[0], crossed(answers_1[1]))
    count = 2 * tok_rows
    leaving_1 = [after(block, *sums_0) for block in leaving_1]
    far_1, pair_1 = (
        [swapped(block[at : at + tok_rows], "expert", 2 * j + 2) for j, block in enumerate(leaving_1)]
        for at in (0, tok_rows)
    )
    back_0 = swapped(near_sum(staying_0, [b[:count] for b in sums_0]), "dp", 1)
    total_0 = far_sums(staying_0, [b[count:] for b in sums_0], back_0)
    far_0 = swapped(total_0[:tok_rows].astype(BF16), "dp", 2)
    def summed(at, blocks):
        return sum([block.astype(F32) for block in blocks], staying_1[at * tok_rows : (at + 1) * tok_rows])

    back_1 = swapped(summed(0, far_1).astype(BF16), "dp", 1)
    rest_1 = [
        swapped(after(block[count:], back_1, *pair_1), "expert", 2 * j + 2) for j, block in enumerate(leaving_1)
    ]
    total_1 = summed(1, pair_1 + [back_1])
    far_1 = swapped(total_1.astype(BF16), "dp", 2)
    back = swapped(summed(2, [block[:tok_rows] for block in rest_1]).astype(BF16), "dp", 1)
    total_1 = summed(3, [block[tok_rows:] for block in rest_1] + [back, far_1])
    total_0 = total_0[tok_rows:] + far_0.astype(F32)
    totals = [passed_along(total.astype(BF16), "segment", 1) for total in (total_0, total_1)]
    return jnp.stack(totals, axis=0)


def solution(mesh):
    return jax.shard_map(
        on_device,
        mesh=mesh,
        in_specs=(
            P(None, ("segment", "expert", "dp"), None),
            P(None, ("segment", "expert", "dp"), None),
            P(None, ("segment", "expert", "dp"), None),
            P(),
            P("segment", "expert", "dp", None),
            P("segment", "expert", "dp", None),
        ),
        out_specs=P(None, ("segment", "expert", "dp"), None),
        check_vma=False,
    )
```

```python
import functools

import jax
import jax.numpy as jnp
from jax import lax
from jax.experimental import pallas as pl
from jax.experimental.pallas import tpu as pltpu
from jax.sharding import PartitionSpec as P

BF16, F32 = jnp.bfloat16, jnp.float32


def passed_along(block, axis, distance):
    devices = range(lax.axis_size(axis))
    route = [((i - distance) % len(devices), i) for i in devices]
    return lax.ppermute(block, axis, route)


def swapped(block, axis, bits):
    return lax.ppermute(block, axis, [(i, i ^ bits) for i in range(lax.axis_size(axis))])


def placed_pairs(routes, expert_home):
    first, second = routes[:, 0], routes[:, 1]
    count = routes.shape[0]
    earlier = jnp.arange(count)[:, None] < jnp.arange(count)[None, :]
    rank_first = jnp.sum(jnp.where(earlier & (first[:, None] == first[None, :]), 1, 0), axis=0)
    rank_second = jnp.sum(
        jnp.where(first[:, None] == second[None, :], 1, 0)
        + jnp.where(earlier & (second[:, None] == second[None, :]), 1, 0),
        axis=0,
    )
    chosen = routes.T
    ids = jnp.arange(expert_home.shape[0], dtype=jnp.int32)
    home = jnp.sum(jnp.where(chosen[:, :, None] == ids, expert_home, 0), axis=-1)
    return home, jnp.stack([rank_first, rank_second])


def arrivals(sides, batch):
    steps = ((0,), (1, 2), (3,)) if batch == 0 else ((0,), (1, 2, 3))
    return [(j, bits) for step in steps for j in range(sides) for bits in step]


def departures(sides, batch):
    order = (3, 1, 2, 0) if batch == 0 else (3, 2, 1, 0)
    return [(j, bits) for j in range(sides) for bits in order]


def plan_kernel(sides, batches, top_count, capacity, half, place_ref, facts_ref, pick_ref, high_ref, low_ref):
    side, core = place_ref[0], place_ref[1]
    tok_rows = facts_ref.shape[-1]
    rows = 2 * half
    tokens = sides * 4 * tok_rows
    padded = -(-rows // 128) * 128
    ids = lax.broadcasted_iota(jnp.int32, (padded, tokens), 0)
    for m in range(batches):
        pick = jnp.zeros((rows, tokens), F32)
        mix = jnp.zeros((padded, tokens), F32)
        for k in range(top_count):
            slots, weights = {}, {}
            for j, bits in departures(sides, m):
                at = m * 2 * top_count + k
                code = facts_ref[j, bits, at : at + 1, :].astype(jnp.int32)
                at = at + top_count
                weights[j, bits] = facts_ref[j, bits, at : at + 1, :]
                home, rank = code // tok_rows, code % tok_rows
                slot = (j * 4 + bits) * capacity + rank + jnp.where(home % 2 == core, 0, half)
                slots[j, bits] = jnp.where(home // 2 == side, slot, -1)
            hit = ids[:rows] == jnp.concatenate([slots[at] for at in arrivals(sides, m)], axis=1)
            pick = jnp.where(hit, 1.0, pick)
            hit = ids == jnp.concatenate([slots[at] for at in departures(sides, m)], axis=1)
            mix = jnp.where(hit, jnp.concatenate([weights[at] for at in departures(sides, m)], axis=1), mix)
        mix = mix.T[:, :rows]
        high = mix.astype(BF16)
        pick_ref[m] = pick.astype(BF16)
        high_ref[m] = high
        low_ref[m] = (mix - high.astype(F32)).astype(BF16)


def plan(place, facts, batches, top_count, capacity, half):
    sides, tok_rows = facts.shape[0], facts.shape[-1]
    shape = jax.ShapeDtypeStruct((batches, 2 * half, sides * 4 * tok_rows), BF16)
    mixed = jax.ShapeDtypeStruct((batches, sides * 4 * tok_rows, 2 * half), BF16)
    vmem = pl.BlockSpec(memory_space=pltpu.VMEM)
    return pl.pallas_call(
        functools.partial(plan_kernel, sides, batches, top_count, capacity, half),
        out_shape=[shape, mixed, mixed],
        in_specs=[pl.BlockSpec(memory_space=pltpu.SMEM), vmem],
        out_specs=[vmem] * 3,
        cost_estimate=pl.CostEstimate(
            flops=10 * shape.size, bytes_accessed=6 * shape.size, transcendentals=0
        ),
        compiler_params=pltpu.CompilerParams(vmem_limit_bytes=32 * 2**20),
    )(place, facts)


def expert_kernel(steps, half, mine_ref, other_ref, up_ref, down_ref, *refs):
    mine_out, other_out, rows, hidden = refs[-4:]
    step = pl.program_id(0)
    chunk = up_ref.shape[0]

    @pl.when(step == 0)
    def _():
        rows[:half] = mine_ref[...]
        rows[half:] = other_ref[...]

    for s in range(steps):

        @pl.when(step == s)
        def _():
            pre_act = lax.dot_general(
                rows[...], up_ref[...], (((1,), (1,)), ((), ())), preferred_element_type=F32
            )
            hidden[:, s * chunk : (s + 1) * chunk] = jax.nn.silu(pre_act).astype(BF16)

    @pl.when(step >= steps)
    def _():
        answer = jnp.dot(hidden[...], down_ref[...], preferred_element_type=F32).astype(BF16)
        mine_out[...] = answer[:half]
        other_out[...] = answer[half:]


def expert_share(mine, other, up_rows, down_rows, *earlier):
    half, features = mine.shape
    units = up_rows.shape[0]
    steps = 4
    chunk, width = units // steps, features // steps
    shape = jax.ShapeDtypeStruct((half, features), BF16)
    whole = pl.BlockSpec((half, features), lambda i: (0, 0))
    part = pl.BlockSpec((half, width), lambda i: (0, jnp.maximum(i - steps, 0)))
    return pl.pallas_call(
        functools.partial(expert_kernel, steps, half),
        grid=(2 * steps,),
        out_shape=[shape] * 2,
        in_specs=[
            whole,
            whole,
            pl.BlockSpec((chunk, features), lambda i: (jnp.minimum(i, steps - 1), 0)),
            pl.BlockSpec((units, width), lambda i: (0, jnp.maximum(i - steps, 0))),
            *[pl.BlockSpec(memory_space=pl.ANY) for _ in earlier],
        ],
        out_specs=[part] * 2,
        scratch_shapes=[pltpu.VMEM((2 * half, features), BF16), pltpu.VMEM((2 * half, units), BF16)],
        cost_estimate=pl.CostEstimate(
            flops=8 * half * units * features,
            bytes_accessed=4 * units * features + 8 * half * features,
            transcendentals=2 * half * units,
        ),
        compiler_params=pltpu.CompilerParams(vmem_limit_bytes=40 * 2**20),
    )(mine, other, up_rows, down_rows, *earlier)


def pack_kernel(count, half, pick_ref, *refs):
    mine_ref, other_ref, group = refs[-3:]
    tok_rows, at = refs[0].shape[-2], 0
    for block in refs[:count]:
        rows = block.shape[-2]
        group[at : at + rows] = block[...].reshape(rows, block.shape[-1])
        at += rows
    chosen = jnp.dot(pick_ref[0], group[...], preferred_element_type=F32).astype(BF16)
    mine_ref[...] = chosen[:half]
    other_ref[...] = chosen[half:]


def pack(m, pick, blocks, *earlier):
    _, rows, tokens = pick.shape
    half, features = rows // 2, blocks[0].shape[-1]
    width = features // 2

    def spec(block):
        if block.ndim == 3:
            return pl.BlockSpec((1, block.shape[1], width), lambda i: (m, 0, i))
        return pl.BlockSpec((block.shape[0], width), lambda i: (0, i))

    return pl.pallas_call(
        functools.partial(pack_kernel, len(blocks), half),
        grid=(features // width,),
        out_shape=[jax.ShapeDtypeStruct((half, features), BF16)] * 2,
        in_specs=[
            pl.BlockSpec((1, rows, tokens), lambda i: (m, 0, 0)),
            *[spec(block) for block in blocks],
            *[pl.BlockSpec(memory_space=pl.ANY) for _ in earlier],
        ],
        out_specs=[pl.BlockSpec((half, width), lambda i: (0, i))] * 2,
        scratch_shapes=[pltpu.VMEM((tokens, width), BF16)],
        cost_estimate=pl.CostEstimate(
            flops=2 * rows * tokens * features,
            bytes_accessed=2 * (rows + tokens) * features + 2 * rows * tokens,
            transcendentals=0,
        ),
        compiler_params=pltpu.CompilerParams(vmem_limit_bytes=32 * 2**20),
    )(pick, *blocks, *earlier)


def unpack_kernel(stays, skipped, mine_ref, other_ref, high_ref, low_ref, *refs):
    refs, answers = refs[skipped:], refs[-1]
    half = mine_ref.shape[0]
    answers[:half] = mine_ref[...]
    answers[half:] = other_ref[...]
    total = None
    for part in (high_ref, low_ref):
        term = jnp.dot(part[0], answers[...], preferred_element_type=F32)
        total = term if total is None else total + term
    refs[0][...] = total[:stays]
    for n, out in enumerate(refs[1:-1]):
        out[...] = total[(n + 1) * stays : (n + 2) * stays].astype(BF16)


def unpack(m, sides, mine, other, high, low, *earlier):
    _, tokens, rows = high.shape
    half, features = mine.shape
    width, stays = features // 2, tokens // sides
    out_shape = [jax.ShapeDtypeStruct((stays, features), F32)]
    out_shape += [jax.ShapeDtypeStruct((stays, features), BF16)] * (sides - 1)
    part = pl.BlockSpec((half, width), lambda i: (0, i))
    whole = pl.BlockSpec((1, tokens, rows), lambda i: (m, 0, 0))
    return pl.pallas_call(
        functools.partial(unpack_kernel, stays, len(earlier)),
        grid=(features // width,),
        out_shape=out_shape,
        in_specs=[part, part, whole, whole, *[pl.BlockSpec(memory_space=pl.ANY) for _ in earlier]],
        out_specs=[pl.BlockSpec((shape.shape[0], width), lambda i: (0, i)) for shape in out_shape],
        scratch_shapes=[pltpu.VMEM((rows, width), BF16)],
        cost_estimate=pl.CostEstimate(
            flops=4 * rows * tokens * features,
            bytes_accessed=2 * (rows + 2 * tokens) * features + 4 * rows * tokens,
            transcendentals=0,
        ),
        compiler_params=pltpu.CompilerParams(vmem_limit_bytes=32 * 2**20),
    )(mine, other, high, low, *earlier)


def after(value, *earlier):
    return lax.optimization_barrier((value,) + earlier)[0] if earlier else value


def on_device(tokens, routes, combine, expert_home, up_weight, down_weight):
    up_rows = up_weight[0, 0]
    down_rows = down_weight[0, 0]
    batches, tok_rows, features = tokens.shape
    top_count = routes.shape[2]
    experts = expert_home.shape[0]
    sides = lax.axis_size("expert") // 2
    capacity = min(tok_rows, tok_rows * top_count // experts + tok_rows // 32)
    here = lax.axis_index("expert")
    place = jnp.stack([here // 2, here % 2]).astype(jnp.int32)
    half = -(-sides * 4 * capacity // 16) * 16

    facts = []
    for m in range(batches):
        home, rank = placed_pairs(routes[m], expert_home)
        facts += [(home * tok_rows + rank).astype(F32), combine[m].T]
    facts = jnp.concatenate(facts)
    facts = jnp.stack([facts] + [swapped(facts, "dp", bits) for bits in (1, 2, 3)])

    def across(block):
        return [swapped(block, "expert", 2 * j) for j in range(1, sides)]

    own_x = across(tokens)
    far, both = [None] * batches, [None] * batches
    pair, pair_x, both_x = [None], [None], [None]
    near = swapped(after(tokens, facts), "dp", 1)
    far[0] = swapped(after(tokens[0], facts), "dp", 2)
    facts_x = jnp.stack([facts] + across(facts))
    pick, high, low = plan(place, facts_x, batches, top_count, capacity, half)
    both[0] = swapped(far[0], "dp", 1)
    pair[0] = jnp.concatenate([near[0], far[0]])
    pair_x[0] = across(after(pair[0], facts_x))
    far[1] = swapped(after(tokens[1], far[0]), "dp", 2)
    both_x[0] = across(both[0])
    both[1] = swapped(far[1], "dp", 1)
    triple = jnp.concatenate([near[1], far[1], both[1]])
    triple_x = across(triple)

    def packed(m, blocks, *earlier):
        mine, other = pack(m, pick, [tokens] + own_x + blocks, *earlier)
        return mine, swapped(other, "expert", 1)

    def crossed(block):
        part = block.shape[0] // 48 * 16
        cuts = [block[at : at + part] for at in range(0, block.shape[0], part)]
        return jnp.concatenate([swapped(cut, "expert", 1) for cut in cuts])

    def unpacked(m, mine, other, *earlier):
        return unpack(m, sides, mine, other, high, low, *earlier)

    def near_sum(staying, first):
        return sum([block.astype(F32) for block in first], staying[: 2 * tok_rows]).astype(BF16)

    def far_sums(staying, second, back):
        return sum([block.astype(F32) for block in second + [back]], staying[2 * tok_rows :])

    rows_0 = packed(0, [pair[0]] + pair_x[0] + [both[0]] + both_x[0], triple)
    answers_0 = expert_share(*rows_0, up_rows, down_rows)
    rows_1 = packed(1, [triple] + triple_x, answers_0[0])
    other = swapped(after(answers_0[1], *triple_x), "expert", 1)
    staying_0, *leaving_0 = unpacked(0, answers_0[0], other)
    sums_0 = [swapped(block, "expert", 2 * j + 2) for j, block in enumerate(leaving_0)]
    answers_1 = expert_share(*rows_1, up_rows, down_rows, leaving_0[0])
    staying_1, *leaving_1 = unpacked(1, answers_1[0], crossed(answers_1[1]))
    count = 2 * tok_rows
    leaving_1 = [after(block, *sums_0) for block in leaving_1]
    far_1, pair_1 = (
        [swapped(block[at : at + tok_rows], "expert", 2 * j + 2) for j, block in enumerate(leaving_1)]
        for at in (0, tok_rows)
    )
    back_0 = swapped(near_sum(staying_0, [b[:count] for b in sums_0]), "dp", 1)
    total_0 = far_sums(staying_0, [b[count:] for b in sums_0], back_0)
    far_0 = swapped(total_0[:tok_rows].astype(BF16), "dp", 2)
    def summed(at, blocks):
        return sum([block.astype(F32) for block in blocks], staying_1[at * tok_rows : (at + 1) * tok_rows])

    back_1 = swapped(summed(0, far_1).astype(BF16), "dp", 1)
    rest_1 = [
        swapped(after(block[count:], back_1, *pair_1), "expert", 2 * j + 2) for j, block in enumerate(leaving_1)
    ]
    total_1 = summed(1, pair_1 + [back_1])
    far_1 = swapped(total_1.astype(BF16), "dp", 2)
    back = swapped(summed(2, [block[:tok_rows] for block in rest_1]).astype(BF16), "dp", 1)
    total_1 = summed(3, [block[tok_rows:] for block in rest_1] + [back, far_1])
    total_0 = total_0[tok_rows:] + far_0.astype(F32)
    totals = [passed_along(total.astype(BF16), "segment", 1) for total in (total_0, total_1)]
    return jnp.stack(totals, axis=0)


def solution(mesh):
    return jax.shard_map(
        on_device,
        mesh=mesh,
        in_specs=(
            P(None, ("segment", "expert", "dp"), None),
            P(None, ("segment", "expert", "dp"), None),
            P(None, ("segment", "expert", "dp"), None),
            P(),
            P("segment", "expert", "dp", None),
            P("segment", "expert", "dp", None),
        ),
        out_specs=P(None, ("segment", "expert", "dp"), None),
        check_vma=False,
    )
```
